32 devices in a mesh: energy: 8 (over z, x), slab: 4 (over y, core).
Axes of the slice: x: 2, y: 2, z: 4, core: 2. Of those that a mesh axis runs over, the one named last changes fastest.
Arguments:
- g_rows: bfloat16 [2, 1536, 4, 64, 384], P(None, 'energy', 'slab'), may hold values from -3 to 3
- injection: bfloat16 [4, 384, 384], P('slab'), may hold values from -0.3125 to 0.3125
- neighbour_ids: int32 [4, 256, 4], P('slab', 'energy'), may hold values from 0 to 5
- coupling: float32 [4, 256, 4], P('slab', 'energy'), may hold values from -4 to 4
Outputs:
- self_energy: bfloat16 [2, 1536, 4, 4096], P(None, 'energy', 'slab')
The draws below stay inside these ranges and needn't reach their ends.
Inputs may be any that keep to these rules, and one draw needn't show every extreme that they name: `neighbour_ids`: an entry v names the neighbour pair in slab offset v // 2 - 1 and at place v % 2 within the tile's group of 2 consecutive tiles.
All inputs are finite; a program needn't handle non-finite values.
Results may differ from the reference program's by a relative error of at most 0.007.
Values may be sent and summed in bfloat16 or wider, within the bound.
A program may use at most 128 MiB of HBM per device.

```python
import jax
import jax.numpy as jnp
from jax import lax

B = 384
NE = 1536
WINDOW = 64
TILE_ENTRIES = 16
GROUP = 2
NEIGHBOURS = 4
SLABS = 4
TILES = 256


def place_ends(values, rng, low, largest):
    longest = values.shape.index(max(values.shape))
    spots = []
    for shift in (0, 1):
        where = [jax.random.randint(jax.random.fold_in(rng, axis), (), 0, length) for axis, length in enumerate(values.shape)]
        where[longest] = (where[longest] + shift) % values.shape[longest]
        spots.append(tuple(where))
    return values.at[spots[0]].set(low).at[spots[1]].set(largest)


def block_scale(key, shape, cuts, least, largest):
    def one(dim, blocks):
        steps = jax.random.uniform(jax.random.fold_in(jax.random.fold_in(key, 6), dim), (blocks,), jnp.float32, least / len(cuts), largest / len(cuts))
        return jnp.repeat(jnp.exp(steps), shape[dim] // blocks).reshape((-1,) + (1,) * (len(shape) - dim - 1))

    level = one(*cuts[0])
    for cut in cuts[1:]:
        level = level * one(*cut)
    return level


def centred(rng, shape, deviation, bound, split=(), dtype=jnp.bfloat16):
    values = jax.random.normal(rng, shape, jnp.float32) * deviation
    if len(split) > 0:
        values = block_scale(rng, shape, split, -0.22, 0.18) * values
    return jnp.clip(values, min=-bound, max=bound).astype(dtype)


def setup_inputs(seed: int = 0) -> dict:
    key_list = jax.random.split(jax.random.key(seed), 5)
    return {
        "g_rows": centred(key_list[0], (2, NE, SLABS, WINDOW, B), 0.19, 3.0, ((1, 8), (2, 4))),
        "injection": centred(key_list[1], (SLABS, B, B), B ** -0.5, 0.3125, ((0, 4),)),
        "neighbour_ids": place_ends(jax.random.randint(key_list[2], (SLABS, TILES, NEIGHBOURS), 0, 3 * GROUP), jax.random.fold_in(key_list[2], 1), 0, (3 * GROUP) - 1).astype(jnp.int32),
        "coupling": centred(key_list[3], (SLABS, TILES, NEIGHBOURS), 0.5, 4.0, ((0, 4), (1, 8)), jnp.float32),
    }


def lesser_slab(pair):
    green_rows, inject = pair
    green_wide = green_rows.astype(jnp.float32)
    scattered = jnp.einsum("xerb,bc->xerc", green_wide, inject.astype(jnp.float32), precision=lax.Precision.HIGHEST)
    scattered = lax.optimization_barrier(scattered.astype(jnp.bfloat16)).astype(jnp.float32)
    real_part = jnp.einsum("erc,esc->ers", scattered[0], green_wide[0], precision=lax.Precision.HIGHEST) + jnp.einsum("erc,esc->ers", scattered[1], green_wide[1], precision=lax.Precision.HIGHEST)
    imag_part = jnp.einsum("erc,esc->ers", scattered[1], green_wide[0], precision=lax.Precision.HIGHEST) - jnp.einsum("erc,esc->ers", scattered[0], green_wide[1], precision=lax.Precision.HIGHEST)
    stacked = jnp.stack([real_part, imag_part]).astype(jnp.bfloat16)
    return stacked.reshape(2, NE, WINDOW * WINDOW)


def convolve_slab(pair):
    lesser, interaction = pair
    lesser_wide = lesser.astype(jnp.float32)
    lesser_wave = jnp.fft.fft(lesser_wide[0] + 1j * lesser_wide[1], n=2 * NE, axis=0)
    inter_wave = jnp.fft.fft(interaction[0] + 1j * interaction[1], n=2 * NE, axis=0)
    series = jnp.fft.ifft(lesser_wave * inter_wave, axis=0)[:NE] * (NE ** -0.5)
    return jnp.stack([jnp.real(series), jnp.imag(series)]).astype(jnp.bfloat16)


def reference(g_rows, injection, neighbour_ids, coupling):
    lesser = lax.map(lesser_slab, (jnp.moveaxis(g_rows, 2, 0), injection))
    tiles = lesser.reshape(SLABS, 2, NE, TILES, TILE_ENTRIES)
    padded = jnp.pad(tiles, ((1, 1), (0, 0), (0, 0), (0, 0), (0, 0)))
    slab_pos = (lax.iota(jnp.int32, SLABS)[:, None, None] + neighbour_ids // GROUP).astype(jnp.int32)
    tile_pos = ((lax.iota(jnp.int32, TILES)[None, :, None] // GROUP) * GROUP + neighbour_ids % GROUP).astype(jnp.int32)
    total = jnp.zeros((SLABS, TILES, 2, NE, TILE_ENTRIES), jnp.float32)
    for k in range(NEIGHBOURS):
        picked = padded[slab_pos[:, :, k], :, :, tile_pos[:, :, k], :]
        total = total + coupling[:, :, k][:, :, None, None, None] * picked.astype(jnp.float32)
    interaction = total.transpose(0, 2, 3, 1, 4).reshape(SLABS, 2, NE, TILES * TILE_ENTRIES)
    result = lax.map(convolve_slab, (lesser, interaction))
    return result.transpose(1, 2, 0, 3)
```

```python
import functools

import jax
import jax.numpy as jnp
import numpy as np
from jax import lax
from jax.experimental import pallas as pl
from jax.experimental.pallas import tpu as pltpu
from jax.sharding import PartitionSpec as P

TILE_ENTRIES = 16
GROUP = 2
RADIX = 8
ROWS = 16
F32 = jnp.float32
BF16 = jnp.bfloat16
HALF_ROOT = 0.5**0.5


def dft_tables(energies):
    total = 2 * energies
    sub = total // RADIX
    j = np.arange(RADIX)[:, None, None]
    k = np.arange(sub)[None, :, None]
    n = np.arange(sub)[None, None, :]
    phase = ((RADIX * k + j) * n % total) * (2.0 * np.pi / total)
    c, s = np.cos(phase), np.sin(phase)
    forward = np.concatenate([np.concatenate([c, s], 2), np.concatenate([-s, c], 2)], 1)
    return forward.astype(np.float32).astype(BF16), forward.transpose(0, 2, 1).astype(np.float32).astype(BF16)


def pair_masks(window):
    side = np.arange(2)
    index = np.arange(window)
    r_side, r_part, r_col = [a.reshape(-1) for a in np.meshgrid(side, side, index, indexing="ij")]
    c_part, c_side, c_col = [a.reshape(-1) for a in np.meshgrid(side, side, index, indexing="ij")]
    same = (r_side[:, None] == c_side[None]) & (r_part[:, None] == c_part[None])
    perm = same & (r_col[:, None] == c_col[None])
    span = GROUP * TILE_ENTRIES
    near = (
        same
        & (r_col[:, None] // span == c_col[None] // span)
        & (r_col[:, None] % TILE_ENTRIES == c_col[None] % TILE_ENTRIES)
    )
    place = r_col[:, None] // TILE_ENTRIES % GROUP
    masks = [near & (place == q) for q in range(GROUP)] + [perm]
    return np.stack(masks).astype(np.float32)


def lesser_kernel(g_ref, inj_ref, out_ref):
    _, count, window, width = g_ref.shape
    g = g_ref[...]
    scattered = jnp.dot(
        g.reshape(2 * count * window, width), inj_ref[...], preferred_element_type=F32
    ).astype(BF16)
    scattered = scattered.reshape(2, count, window, width)
    left = jnp.concatenate([scattered[0], scattered[1]], axis=-1)
    right = jnp.concatenate(
        [jnp.concatenate([g[0], g[1]], axis=-1), jnp.concatenate([-g[1], g[0]], axis=-1)], axis=1
    )
    full = lax.dot_general(
        left, right, (((2,), (2,)), ((0,), (0,))), preferred_element_type=F32
    )
    out_ref[...] = jnp.swapaxes(full, 0, 1).astype(BF16)


def lesser_call(green, inject):
    _, count, window, width = green.shape
    block = 16
    return pl.pallas_call(
        lesser_kernel,
        grid=(count // block,),
        in_specs=[
            pl.BlockSpec((2, block, window, width), lambda i: (0, i, 0, 0)),
            pl.BlockSpec((width, width), lambda i: (0, 0)),
        ],
        out_specs=pl.BlockSpec((window, block, 2 * window), lambda i: (0, i, 0)),
        out_shape=jax.ShapeDtypeStruct((window, count, 2 * window), BF16),
        compiler_params=pltpu.CompilerParams(vmem_limit_bytes=48 * 2**20),
        cost_estimate=pl.CostEstimate(
            flops=2 * count * window * width * (2 * width + 4 * window),
            bytes_accessed=2 * 2 * count * window * (width + window),
            transcendentals=0,
        ),
        name="lesser",
    )(green, inject)


def mix(own, before, after, mask_ref, weight, z_ref, pair, pairs):
    half = own.shape[1] // 2
    total = None
    for o, x in enumerate((before, own, after)):
        m = mask_ref[0] * weight(o, 0) + mask_ref[1] * weight(o, 1)
        term = jnp.dot(x, m.astype(BF16), preferred_element_type=F32)
        total = term if total is None else total + term
    same = jnp.dot(own, mask_ref[2].astype(BF16), preferred_element_type=F32)
    for part in range(2):
        lanes = slice(part * half, (part + 1) * half)
        z_ref[part, :, pair * half : (pair + 1) * half] = same[:, lanes]
        z_ref[part, :, (pairs + pair) * half : (pairs + pair + 1) * half] = total[:, lanes]


def convolve(z_ref, fwd_ref, inv_ref, t_ref, v_ref, store, scale):
    _, energies, wide = z_ref.shape
    cols = wide // 2
    sub = 2 * energies // RADIX
    c = HALF_ROOT

    def split(i, carry):
        row = pl.multiple_of(i * ROWS, ROWS)
        for lane in range(0, wide, 256):
            lanes = pl.ds(lane, 256)
            re = [z_ref[0, pl.ds(b * sub + row, ROWS), lanes] for b in range(4)]
            im = [z_ref[1, pl.ds(b * sub + row, ROWS), lanes] for b in range(4)]

            def put(j, a, b):
                t_ref[j, pl.ds(row, ROWS), lanes] = a.astype(BF16)
                t_ref[j, pl.ds(sub + row, ROWS), lanes] = b.astype(BF16)

            def four(j, r, m):
                s0r, s0m, d0r, d0m = r[0] + r[2], m[0] + m[2], r[0] - r[2], m[0] - m[2]
                s1r, s1m, d1r, d1m = r[1] + r[3], m[1] + m[3], r[1] - r[3], m[1] - m[3]
                put(j, s0r + s1r, s0m + s1m)
                put(j + 2, d0r + d1m, d0m - d1r)
                put(j + 4, s0r - s1r, s0m - s1m)
                put(j + 6, d0r - d1m, d0m + d1r)

            four(0, re, im)
            tr = [re[0], (re[1] + im[1]) * c, im[2], (im[3] - re[3]) * c]
            tm = [im[0], (im[1] - re[1]) * c, -re[2], -(im[3] + re[3]) * c]
            four(1, tr, tm)
        return carry

    lax.fori_loop(0, sub // ROWS, split, 0)

    def spectral(j, carry):
        x = jnp.dot(fwd_ref[j], t_ref[j], preferred_element_type=F32)
        lr, li = x[:sub, :cols], x[sub:, :cols]
        ir, ii = x[:sub, cols:], x[sub:, cols:]
        p = jnp.concatenate([lr * ir - li * ii, lr * ii + li * ir], axis=0).astype(BF16)
        v_ref[j] = jnp.dot(inv_ref[j], p, preferred_element_type=F32)
        return carry

    lax.fori_loop(0, RADIX, spectral, 0)

    def gather(i, carry):
        row = pl.multiple_of(i * ROWS, ROWS)
        vr = [v_ref[j, pl.ds(row, ROWS), :] for j in range(RADIX)]
        vm = [v_ref[j, pl.ds(sub + row, ROWS), :] for j in range(RADIX)]

        def four(j):
            r, m = vr[j::2], vm[j::2]
            s0r, s0m, d0r, d0m = r[0] + r[2], m[0] + m[2], r[0] - r[2], m[0] - m[2]
            s1r, s1m, d1r, d1m = r[1] + r[3], m[1] + m[3], r[1] - r[3], m[1] - m[3]
            return (
                [s0r + s1r, d0r - d1m, s0r - s1r, d0r + d1m],
                [s0m + s1m, d0m + d1r, s0m - s1m, d0m - d1r],
            )

        er, em = four(0)
        ar, am = four(1)
        br = [ar[0], (ar[1] - am[1]) * c, -am[2], -(ar[3] + am[3]) * c]
        bm = [am[0], (ar[1] + am[1]) * c, ar[2], (ar[3] - am[3]) * c]
        for b in range(4):
            store(b * sub + row, (er[b] + br[b]) * scale, (em[b] + bm[b]) * scale)
        return carry

    lax.fori_loop(0, sub // ROWS, gather, 0)


def convolve_kernel(x_ref, lo_ref, hi_ref, w_ref, mask_ref, fwd_ref, inv_ref, out_ref, z_ref, t_ref, v_ref):
    devices, rows, count, lanes = x_ref.shape
    energies = devices * count
    pairs = rows // 2

    def both(ref, p):
        parts = [ref[:, 2 * p + a].reshape(energies, lanes) for a in range(2)]
        return jnp.concatenate(parts, axis=1)

    for p in range(pairs):
        mix(
            both(x_ref, p),
            both(lo_ref, p),
            both(hi_ref, p),
            mask_ref,
            lambda o, q: w_ref[p, pl.ds(o * 2 + q, 1), :],
            z_ref,
            p,
            pairs,
        )

    def store(row, real, imag):
        dest = row // count
        inside = pl.multiple_of(row % count, ROWS)
        out_ref[dest, 0, pl.ds(inside, ROWS), :] = real.astype(BF16)
        out_ref[dest, 1, pl.ds(inside, ROWS), :] = imag.astype(BF16)

    scale = energies**-0.5 / (2 * energies)
    convolve(z_ref, fwd_ref, inv_ref, t_ref, v_ref, store, scale)


def convolve_call(x, lo, hi, w, masks, fwd, inv):
    devices, rows, count, lanes = x.shape
    energies = devices * count
    cols = rows * lanes // 2
    sub = 2 * energies // RADIX
    vmem = pl.BlockSpec(memory_space=pltpu.VMEM)
    return pl.pallas_call(
        convolve_kernel,
        in_specs=[vmem] * 7,
        out_specs=vmem,
        out_shape=jax.ShapeDtypeStruct((devices, 2, count, cols), BF16),
        scratch_shapes=[
            pltpu.VMEM((2, energies, 2 * cols), F32),
            pltpu.VMEM((RADIX, 2 * sub, 2 * cols), BF16),
            pltpu.VMEM((RADIX, 2 * sub, cols), F32),
        ],
        compiler_params=pltpu.CompilerParams(vmem_limit_bytes=60 * 2**20),
        cost_estimate=pl.CostEstimate(
            flops=2 * RADIX * 4 * sub * sub * 3 * cols, bytes_accessed=24 * 2**20, transcendentals=0
        ),
        name="convolve",
    )(x, lo, hi, w, masks, fwd, inv)


def pair_weights(neighbour_ids, coupling, window):
    tiles = neighbour_ids.shape[0]
    candidates = lax.iota(jnp.int32, 3 * GROUP)
    matches = (neighbour_ids[:, :, None] == candidates).astype(F32)
    weights = jnp.sum(matches * coupling[:, :, None], axis=1)
    per_pair = 2 * window // TILE_ENTRIES
    weights = weights.reshape(tiles // per_pair, per_pair, 3 * GROUP).transpose(0, 2, 1)
    lanes = jnp.repeat(weights, TILE_ENTRIES, axis=2)
    lanes = jnp.concatenate([lanes, lanes], axis=2)
    return jnp.pad(lanes, ((0, 0), (0, 2), (0, 0)))


def local(g_rows, injection, neighbour_ids, coupling):
    green = g_rows[:, :, 0]
    devices = lax.axis_size("energy")
    slabs = lax.axis_size("slab")
    window = green.shape[2]
    count = green.shape[1]
    energies = devices * count
    rows = window // devices
    lesser = lesser_call(green, injection[0]).reshape(devices, rows, count, 2 * window)
    weights = pair_weights(neighbour_ids[0], coupling[0], window)
    masks = jnp.asarray(pair_masks(window))
    fwd, inv = (jnp.asarray(t) for t in dft_tables(energies))
    chunks = max(1, rows // 4)
    step = rows // chunks
    up = [(i, i + 1) for i in range(slabs - 1)]
    down = [(i + 1, i) for i in range(slabs - 1)]
    results = []
    for c in range(chunks):
        x = lax.all_to_all(lesser[:, c * step : (c + 1) * step], "energy", 0, 0, tiled=True)
        lo = lax.ppermute(x, "slab", up)
        hi = lax.ppermute(x, "slab", down)
        w = weights[c * step // 2 : (c + 1) * step // 2]
        y = convolve_call(x, lo, hi, w, masks, fwd, inv)
        results.append(lax.all_to_all(y, "energy", 0, 0, tiled=True))
    out = jnp.stack(results, axis=1)
    out = out.transpose(2, 3, 0, 1, 4).reshape(2, count, 1, window * window)
    return out


def solution(mesh):
    in_specs = (
        P(None, "energy", "slab", None, None),
        P("slab", None, None),
        P("slab", "energy", None),
        P("slab", "energy", None),
    )
    out_specs = P(None, "energy", "slab", None)
    return jax.shard_map(local, mesh=mesh, in_specs=in_specs, out_specs=out_specs, check_vma=False)
```

```python
import functools

import jax
import jax.numpy as jnp
import numpy as np
from jax import lax
from jax.experimental import pallas as pl
from jax.experimental.pallas import tpu as pltpu
from jax.sharding import PartitionSpec as P

TILE_ENTRIES = 16
GROUP = 2
RADIX = 8
ROWS = 16
F32 = jnp.float32
BF16 = jnp.bfloat16
HALF_ROOT = 0.5**0.5
MESH = pl.DeviceIdType.MESH


def dft_tables(energies):
    total = 2 * energies
    sub = total // RADIX
    j = np.arange(RADIX)[:, None, None]
    k = np.arange(sub)[None, :, None]
    n = np.arange(sub)[None, None, :]
    phase = ((RADIX * k + j) * n % total) * (2.0 * np.pi / total)
    c, s = np.cos(phase), np.sin(phase)
    forward = np.concatenate([np.concatenate([c, s], 2), np.concatenate([-s, c], 2)], 1)
    return forward.astype(np.float32).astype(BF16), forward.transpose(0, 2, 1).astype(np.float32).astype(BF16)


def pair_masks(window):
    side = np.arange(2)
    index = np.arange(window)
    r_side, r_part, r_col = [a.reshape(-1) for a in np.meshgrid(side, side, index, indexing="ij")]
    c_part, c_side, c_col = [a.reshape(-1) for a in np.meshgrid(side, side, index, indexing="ij")]
    same = (r_side[:, None] == c_side[None]) & (r_part[:, None] == c_part[None])
    perm = same & (r_col[:, None] == c_col[None])
    span = GROUP * TILE_ENTRIES
    near = (
        same
        & (r_col[:, None] // span == c_col[None] // span)
        & (r_col[:, None] % TILE_ENTRIES == c_col[None] % TILE_ENTRIES)
    )
    place = r_col[:, None] // TILE_ENTRIES % GROUP
    masks = [near & (place == q) for q in range(GROUP)] + [perm]
    return np.stack(masks).astype(np.float32)


def lesser_block(g, inject):
    _, count, window, width = g.shape
    scattered = jnp.dot(
        g.reshape(2 * count * window, width), inject, preferred_element_type=F32
    ).astype(BF16)
    scattered = scattered.reshape(2, count, window, width)
    left = jnp.concatenate([scattered[0], scattered[1]], axis=-1)
    right = jnp.concatenate(
        [jnp.concatenate([g[0], g[1]], axis=-1), jnp.concatenate([-g[1], g[0]], axis=-1)], axis=1
    )
    full = lax.dot_general(
        left, right, (((2,), (2,)), ((0,), (0,))), preferred_element_type=F32
    )
    return jnp.swapaxes(full, 0, 1).astype(BF16)


def mix(own, before, after, mask_ref, weight, z_ref):
    half = own.shape[1] // 2
    total = None
    for o, x in enumerate((before, own, after)):
        m = mask_ref[0] * weight(o, 0) + mask_ref[1] * weight(o, 1)
        term = jnp.dot(x, m.astype(BF16), preferred_element_type=F32)
        total = term if total is None else total + term
    same = jnp.dot(own, mask_ref[2].astype(BF16), preferred_element_type=F32)
    for part in range(2):
        lanes = slice(part * half, (part + 1) * half)
        z_ref[part, :, :half] = same[:, lanes]
        z_ref[part, :, half:] = total[:, lanes]


def split_pair(z_ref, t_ref, pair, pairs):
    _, energies, wide = z_ref.shape
    half = wide // 2
    sub = 2 * energies // RADIX
    c = HALF_ROOT

    def split(i, carry):
        row = pl.multiple_of(i * ROWS, ROWS)
        for part in range(2):
            lanes = slice(part * half, (part + 1) * half)
            to = part * pairs * half + pair * half
            to = slice(to, to + half)
            re = [z_ref[0, pl.ds(b * sub + row, ROWS), lanes] for b in range(4)]
            im = [z_ref[1, pl.ds(b * sub + row, ROWS), lanes] for b in range(4)]

            def put(j, a, b):
                t_ref[j, pl.ds(row, ROWS), to] = a.astype(BF16)
                t_ref[j, pl.ds(sub + row, ROWS), to] = b.astype(BF16)

            def four(j, r, m):
                s0r, s0m, d0r, d0m = r[0] + r[2], m[0] + m[2], r[0] - r[2], m[0] - m[2]
                s1r, s1m, d1r, d1m = r[1] + r[3], m[1] + m[3], r[1] - r[3], m[1] - m[3]
                put(j, s0r + s1r, s0m + s1m)
                put(j + 2, d0r + d1m, d0m - d1r)
                put(j + 4, s0r - s1r, s0m - s1m)
                put(j + 6, d0r - d1m, d0m + d1r)

            four(0, re, im)
            tr = [re[0], (re[1] + im[1]) * c, im[2], (im[3] - re[3]) * c]
            tm = [im[0], (im[1] - re[1]) * c, -re[2], -(im[3] + re[3]) * c]
            four(1, tr, tm)
        return carry

    lax.fori_loop(0, sub // ROWS, split, 0)

def convolve(t_ref, fwd_ref, inv_ref, v_ref, store, scale, hooks):
    _, double, wide = t_ref.shape
    cols = wide // 2
    sub = double // 2
    c = HALF_ROOT

    def spectral(j, carry):
        x = jnp.dot(fwd_ref[j], t_ref[j], preferred_element_type=F32)
        lr, li = x[:sub, :cols], x[sub:, :cols]
        ir, ii = x[:sub, cols:], x[sub:, cols:]
        p = jnp.concatenate([lr * ir - li * ii, lr * ii + li * ir], axis=0).astype(BF16)
        v_ref[j] = jnp.dot(inv_ref[j], p, preferred_element_type=F32)
        return carry

    stage = RADIX // max(1, len(hooks))
    for start in range(0, RADIX, stage):
        lax.fori_loop(start, start + stage, spectral, 0)
        if hooks:
            hooks[start // stage]()

    def gather(i, carry):
        row = pl.multiple_of(i * ROWS, ROWS)
        vr = [v_ref[j, pl.ds(row, ROWS), :] for j in range(RADIX)]
        vm = [v_ref[j, pl.ds(sub + row, ROWS), :] for j in range(RADIX)]

        def four(j):
            r, m = vr[j::2], vm[j::2]
            s0r, s0m, d0r, d0m = r[0] + r[2], m[0] + m[2], r[0] - r[2], m[0] - m[2]
            s1r, s1m, d1r, d1m = r[1] + r[3], m[1] + m[3], r[1] - r[3], m[1] - m[3]
            return (
                [s0r + s1r, d0r - d1m, s0r - s1r, d0r + d1m],
                [s0m + s1m, d0m + d1r, s0m - s1m, d0m - d1r],
            )

        er, em = four(0)
        ar, am = four(1)
        br = [ar[0], (ar[1] - am[1]) * c, -am[2], -(ar[3] + am[3]) * c]
        bm = [am[0], (ar[1] + am[1]) * c, ar[2], (ar[3] - am[3]) * c]
        for b in range(4):
            store(b * sub + row, (er[b] + br[b]) * scale, (em[b] + bm[b]) * scale)
        return carry

    lax.fori_loop(0, sub // ROWS, gather, 0)


def fused_kernel(
    g_ref, inj_ref, w_ref, mask_ref, fwd_hbm, inv_hbm, out_ref,
    g_buf, send, rx, lo, hi, y, fwd, inv, z, t, v,
    g_sem, tab_sem, own_sem, a_send, a_recv, up_send, up_recv, down_send, down_recv,
    ret_own, ret_send, ret_recv,
):
    chunks, devices, rows, count, lanes = rx.shape
    energies = devices * count
    pairs = rows // 2
    cols = rows * lanes // 2
    block = g_buf.shape[2]
    groups = a_send.shape[1]
    span = count // groups
    me = lax.axis_index("energy")
    slab = lax.axis_index("slab")
    slabs = lax.axis_size("slab")
    has_up = slab < slabs - 1
    has_down = slab > 0

    def g_copy(i):
        start = pl.multiple_of(i * block, block)
        return pltpu.make_async_copy(
            g_ref.at[:, pl.ds(start, block)], g_buf.at[i % 2], g_sem.at[i % 2]
        )

    g_copy(0).start()
    fwd_copy = pltpu.make_async_copy(fwd_hbm, fwd, tab_sem.at[0])
    inv_copy = pltpu.make_async_copy(inv_hbm, inv, tab_sem.at[1])

    barrier = pltpu.get_barrier_semaphore()

    def greet(k, carry):
        pl.semaphore_signal(
            barrier, inc=1, device_id=((me + k) % devices, slab), device_id_type=MESH
        )
        return carry

    lax.fori_loop(1, devices, greet, 0)

    @pl.when(has_up)
    def _():
        pl.semaphore_signal(barrier, inc=1, device_id=(me, slab + 1), device_id_type=MESH)

    @pl.when(has_down)
    def _():
        pl.semaphore_signal(barrier, inc=1, device_id=(me, slab - 1), device_id_type=MESH)

    peers = devices - 1 + jnp.where(has_up, 1, 0) + jnp.where(has_down, 1, 0)
    pl.semaphore_wait(barrier, peers)

    def when_range(g):
        return pl.ds(pl.multiple_of(g * span, ROWS), span)

    def tile_copy(c, g, source, target, peer):
        part = when_range(g)
        return pltpu.make_async_remote_copy(
            src_ref=send.at[target, c * rows : (c + 1) * rows, part],
            dst_ref=rx.at[c, source, :, part],
            send_sem=a_send.at[c, g, target],
            recv_sem=a_recv.at[c, g, source],
            device_id=(peer, slab),
            device_id_type=MESH,
        )

    def own_copy(c, g):
        part = when_range(g)
        return pltpu.make_async_copy(
            send.at[me, c * rows : (c + 1) * rows, part], rx.at[c, me, :, part], own_sem.at[c, g]
        )

    def send_group(c, g):
        def one(k, carry):
            to = (me + k) % devices
            tile_copy(c, g, me, to, to).start()
            return carry

        lax.fori_loop(1, devices, one, 0)
        own_copy(c, g).start()

    def halo_copy(c, g, up):
        part = when_range(g)
        return pltpu.make_async_remote_copy(
            src_ref=rx.at[c, :, :, part],
            dst_ref=(lo if up else hi).at[c, :, :, part],
            send_sem=(up_send if up else down_send).at[c, g],
            recv_sem=(up_recv if up else down_recv).at[c, g],
            device_id=(me, slab + 1 if up else slab - 1),
            device_id_type=MESH,
        )

    def forward_group(c, g):
        def one(k, carry):
            source = (me + devices - k) % devices
            tile_copy(c, g, source, source, source).wait_recv()
            return carry

        lax.fori_loop(1, devices, one, 0)
        own_copy(c, g).wait()

        @pl.when(has_up)
        def _():
            halo_copy(c, g, True).start()

        @pl.when(has_down)
        def _():
            halo_copy(c, g, False).start()

    def wait_halos(c):
        def one(g, carry):
            @pl.when(has_down)
            def _():
                halo_copy(c, g, True).wait_recv()

            @pl.when(has_up)
            def _():
                halo_copy(c, g, False).wait_recv()

            return carry

        lax.fori_loop(0, groups, one, 0)

    steps = span // block

    def lesser_group(g, carry):
        def step(b, inner):
            i = g * steps + b

            @pl.when(i + 1 < groups * steps)
            def _():
                g_copy(i + 1).start()

            g_copy(i).wait()
            result = lesser_block(g_buf[i % 2], inj_ref[...])
            start = pl.multiple_of(i * block, block)
            send[:, :, pl.ds(start, block), :] = result.reshape(
                devices, chunks * rows, block, lanes
            )
            return inner

        lax.fori_loop(0, steps, step, 0)
        send_group(0, g)

        @pl.when(g > 0)
        def _():
            forward_group(0, g - 1)

        return carry

    @pl.when(slab == 0)
    def _():
        lo[...] = jnp.zeros_like(lo)

    @pl.when(slab == slabs - 1)
    def _():
        hi[...] = jnp.zeros_like(hi)

    fwd_copy.start()
    inv_copy.start()
    lax.fori_loop(0, groups, lesser_group, 0)
    for c in range(1, chunks):
        lax.fori_loop(0, groups, lambda g, carry: (send_group(c, g), carry)[1], 0)
    forward_group(0, groups - 1)
    fwd_copy.wait()
    inv_copy.wait()

    def both(ref, c, p):
        parts = [ref[c, :, 2 * p + a].reshape(energies, lanes) for a in range(2)]
        return jnp.concatenate(parts, axis=1)

    def return_copy(c, source, target, peer):
        at = pl.multiple_of(source * (chunks * cols) + c * cols, 128)
        return pltpu.make_async_remote_copy(
            src_ref=y.at[c, target],
            dst_ref=out_ref.at[:, :, pl.ds(at, cols)],
            send_sem=ret_send.at[c, target],
            recv_sem=ret_recv.at[c, source],
            device_id=(peer, slab),
            device_id_type=MESH,
        )

    def return_own(c):
        at = pl.multiple_of(me * (chunks * cols) + c * cols, 128)
        return pltpu.make_async_copy(
            y.at[c, me], out_ref.at[:, :, pl.ds(at, cols)], ret_own.at[c]
        )

    scale = energies**-0.5 / (2 * energies)
    for c in range(chunks):
        wait_halos(c)
        for p in range(pairs):
            mix(
                both(rx, c, p),
                both(lo, c, p),
                both(hi, c, p),
                mask_ref,
                lambda o, q: w_ref[c * pairs + p, pl.ds(o * 2 + q, 1), :],
                z,
            )
            split_pair(z, t, p, pairs)

        def store(row, real, imag):
            dest = row // count
            inside = pl.multiple_of(row % count, ROWS)
            y[c, dest, 0, pl.ds(inside, ROWS), :] = real.astype(BF16)
            y[c, dest, 1, pl.ds(inside, ROWS), :] = imag.astype(BF16)

        hooks = []
        if c + 1 < chunks:
            hooks = [functools.partial(forward_group, c + 1, g) for g in range(groups)]
        convolve(t, fwd, inv, v, store, scale, hooks)

        def give(k, carry):
            to = (me + k) % devices
            return_copy(c, me, to, to).start()
            return carry

        lax.fori_loop(1, devices, give, 0)
        return_own(c).start()

    for c in range(chunks):
        return_own(c).wait()

        def finish(k, carry):
            peer = (me + k) % devices
            return_copy(c, peer, peer, peer).wait()
            return carry

        lax.fori_loop(1, devices, finish, 0)

        def drain(g, carry):
            def one(k, inner):
                to = (me + k) % devices
                tile_copy(c, g, me, to, to).wait_send()
                return inner

            lax.fori_loop(1, devices, one, 0)

            @pl.when(has_up)
            def _():
                halo_copy(c, g, True).wait_send()

            @pl.when(has_down)
            def _():
                halo_copy(c, g, False).wait_send()

            return carry

        lax.fori_loop(0, groups, drain, 0)


def fused_call(green, inject, weights, masks, fwd, inv, devices):
    _, count, window, width = green.shape
    energies = devices * count
    local_rows = window // devices
    chunks = max(1, local_rows // 4)
    rows = local_rows // chunks
    lanes = 2 * window
    cols = rows * lanes // 2
    sub = 2 * energies // RADIX
    groups = max(1, count // 48)
    vmem = pl.BlockSpec(memory_space=pltpu.VMEM)
    hbm = pl.BlockSpec(memory_space=pl.ANY)
    dma = pltpu.SemaphoreType.DMA
    slots = pltpu.VMEM((chunks, devices, rows, count, lanes), BF16)
    return pl.pallas_call(
        fused_kernel,
        in_specs=[hbm, vmem, vmem, vmem, hbm, hbm],
        out_specs=hbm,
        out_shape=jax.ShapeDtypeStruct((2, count, window * window), BF16),
        scratch_shapes=[
            pltpu.VMEM((2, 2, ROWS, window, width), BF16),
            pltpu.VMEM((devices, local_rows, count, lanes), BF16),
            slots,
            slots,
            slots,
            pltpu.VMEM((chunks, devices, 2, count, cols), BF16),
            pltpu.VMEM(fwd.shape, BF16),
            pltpu.VMEM(inv.shape, BF16),
            pltpu.VMEM((2, energies, 2 * lanes), F32),
            pltpu.VMEM((RADIX, 2 * sub, 2 * cols), BF16),
            pltpu.VMEM((RADIX, 2 * sub, cols), F32),
            dma((2,)),
            dma((2,)),
            dma((chunks, groups)),
            dma((chunks, groups, devices)),
            dma((chunks, groups, devices)),
            dma((chunks, groups)),
            dma((chunks, groups)),
            dma((chunks, groups)),
            dma((chunks, groups)),
            dma((chunks,)),
            dma((chunks, devices)),
            dma((chunks, devices)),
        ],
        compiler_params=pltpu.CompilerParams(
            vmem_limit_bytes=63 * 2**20, collective_id=0, has_side_effects=True
        ),
        cost_estimate=pl.CostEstimate(
            flops=2 * count * window * width * (2 * width + 4 * window)
            + 2 * RADIX * 4 * sub * sub * 3 * cols * chunks,
            bytes_accessed=48 * 2**20,
            transcendentals=0,
        ),
        name="fused",
    )(green, inject, weights, masks, fwd, inv)


def pair_weights(neighbour_ids, coupling, window):
    tiles = neighbour_ids.shape[0]
    candidates = lax.iota(jnp.int32, 3 * GROUP)
    matches = (neighbour_ids[:, :, None] == candidates).astype(F32)
    weights = jnp.sum(matches * coupling[:, :, None], axis=1)
    per_pair = 2 * window // TILE_ENTRIES
    weights = weights.reshape(tiles // per_pair, per_pair, 3 * GROUP).transpose(0, 2, 1)
    lanes = jnp.repeat(weights, TILE_ENTRIES, axis=2)
    lanes = jnp.concatenate([lanes, lanes], axis=2)
    return jnp.pad(lanes, ((0, 0), (0, 2), (0, 0)))


def local(g_rows, injection, neighbour_ids, coupling):
    green = g_rows[:, :, 0]
    devices = lax.axis_size("energy")
    window = green.shape[2]
    count = green.shape[1]
    weights = pair_weights(neighbour_ids[0], coupling[0], window)
    masks = jnp.asarray(pair_masks(window))
    fwd, inv = (jnp.asarray(t) for t in dft_tables(devices * count))
    out = fused_call(green, injection[0], weights, masks, fwd, inv, devices)
    return out.reshape(2, count, 1, window * window)


def solution(mesh):
    in_specs = (
        P(None, "energy", "slab", None, None),
        P("slab", None, None),
        P("slab", "energy", None),
        P("slab", "energy", None),
    )
    out_specs = P(None, "energy", "slab", None)
    return jax.shard_map(local, mesh=mesh, in_specs=in_specs, out_specs=out_specs, check_vma=False)
```

```python
import functools

import jax
import jax.numpy as jnp
import numpy as np
from jax import lax
from jax.experimental import pallas as pl
from jax.experimental.pallas import tpu as pltpu
from jax.sharding import PartitionSpec as P

TILE_ENTRIES = 16
GROUP = 2
RADIX = 8
ROWS = 16
F32 = jnp.float32
BF16 = jnp.bfloat16
HALF_ROOT = 0.5**0.5
MESH = pl.DeviceIdType.MESH


def dft_tables(energies):
    total = 2 * energies
    sub = total // RADIX
    j = np.arange(RADIX)[:, None, None]
    k = np.arange(sub)[None, :, None]
    n = np.arange(sub)[None, None, :]
    phase = ((RADIX * k + j) * n % total) * (2.0 * np.pi / total)
    c, s = np.cos(phase), np.sin(phase)
    forward = np.concatenate([np.concatenate([c, s], 2), np.concatenate([-s, c], 2)], 1)
    return forward.astype(np.float32).astype(BF16), forward.transpose(0, 2, 1).astype(np.float32).astype(BF16)


def pair_masks(window):
    side = np.arange(2)
    index = np.arange(window)
    r_side, r_part, r_col = [a.reshape(-1) for a in np.meshgrid(side, side, index, indexing="ij")]
    c_part, c_side, c_col = [a.reshape(-1) for a in np.meshgrid(side, side, index, indexing="ij")]
    same = (r_side[:, None] == c_side[None]) & (r_part[:, None] == c_part[None])
    perm = same & (r_col[:, None] == c_col[None])
    span = GROUP * TILE_ENTRIES
    near = (
        same
        & (r_col[:, None] // span == c_col[None] // span)
        & (r_col[:, None] % TILE_ENTRIES == c_col[None] % TILE_ENTRIES)
    )
    place = r_col[:, None] // TILE_ENTRIES % GROUP
    masks = [near & (place == q) for q in range(GROUP)] + [perm]
    return np.stack(masks).astype(np.float32)


def lesser_block(g, inject):
    _, count, window, width = g.shape
    scattered = jnp.dot(
        g.reshape(2 * count * window, width), inject, preferred_element_type=F32
    ).astype(BF16)
    scattered = scattered.reshape(2, count, window, width)
    left = jnp.concatenate([scattered[0], scattered[1]], axis=-1)
    right = jnp.concatenate(
        [jnp.concatenate([g[0], g[1]], axis=-1), jnp.concatenate([-g[1], g[0]], axis=-1)], axis=1
    )
    full = lax.dot_general(
        left, right, (((2,), (2,)), ((0,), (0,))), preferred_element_type=F32
    )
    return jnp.swapaxes(full, 0, 1).astype(BF16)


def mix(own, before, after, mask_ref, weight, z_ref):
    half = own.shape[1] // 2
    blocks = [mask_ref[0] * weight(o, 0) + mask_ref[1] * weight(o, 1) for o in range(3)]
    total = jnp.dot(
        jnp.concatenate([before, own, after], axis=1),
        jnp.concatenate(blocks, axis=0).astype(BF16),
        preferred_element_type=F32,
    )
    same = jnp.dot(own, mask_ref[2].astype(BF16), preferred_element_type=F32)
    for part in range(2):
        lanes = slice(part * half, (part + 1) * half)
        z_ref[part, :, :half] = same[:, lanes]
        z_ref[part, :, half:] = total[:, lanes]


def split_pair(z_ref, t_ref, pair, pairs):
    _, energies, wide = z_ref.shape
    half = wide // 2
    sub = 2 * energies // RADIX
    c = HALF_ROOT

    def split(i, carry):
        row = pl.multiple_of(i * ROWS, ROWS)
        for part in range(2):
            lanes = slice(part * half, (part + 1) * half)
            to = part * pairs * half + pair * half
            to = slice(to, to + half)
            re = [z_ref[0, pl.ds(b * sub + row, ROWS), lanes] for b in range(4)]
            im = [z_ref[1, pl.ds(b * sub + row, ROWS), lanes] for b in range(4)]

            def put(j, a, b):
                t_ref[j, pl.ds(row, ROWS), to] = a.astype(BF16)
                t_ref[j, pl.ds(sub + row, ROWS), to] = b.astype(BF16)

            def four(j, r, m):
                s0r, s0m, d0r, d0m = r[0] + r[2], m[0] + m[2], r[0] - r[2], m[0] - m[2]
                s1r, s1m, d1r, d1m = r[1] + r[3], m[1] + m[3], r[1] - r[3], m[1] - m[3]
                put(j, s0r + s1r, s0m + s1m)
                put(j + 2, d0r + d1m, d0m - d1r)
                put(j + 4, s0r - s1r, s0m - s1m)
                put(j + 6, d0r - d1m, d0m + d1r)

            four(0, re, im)
            tr = [re[0], (re[1] + im[1]) * c, im[2], (im[3] - re[3]) * c]
            tm = [im[0], (im[1] - re[1]) * c, -re[2], -(im[3] + re[3]) * c]
            four(1, tr, tm)
        return carry

    lax.fori_loop(0, sub // ROWS, split, 0)

def convolve(t_ref, fwd_ref, inv_ref, v_ref, store, scale, hooks):
    _, double, wide = t_ref.shape
    cols = wide // 2
    sub = double // 2
    c = HALF_ROOT

    def spectral(j, carry):
        x = jnp.dot(fwd_ref[j], t_ref[j], preferred_element_type=F32)
        lr, li = x[:sub, :cols], x[sub:, :cols]
        ir, ii = x[:sub, cols:], x[sub:, cols:]
        p = jnp.concatenate([lr * ir - li * ii, lr * ii + li * ir], axis=0).astype(BF16)
        v_ref[j] = jnp.dot(inv_ref[j], p, preferred_element_type=F32)
        return carry

    stage = RADIX // max(1, len(hooks))
    for start in range(0, RADIX, stage):
        lax.fori_loop(start, start + stage, spectral, 0)
        if hooks:
            hooks[start // stage]()

    def gather(i, carry):
        row = pl.multiple_of(i * ROWS, ROWS)
        vr = [v_ref[j, pl.ds(row, ROWS), :] for j in range(RADIX)]
        vm = [v_ref[j, pl.ds(sub + row, ROWS), :] for j in range(RADIX)]

        def four(j):
            r, m = vr[j::2], vm[j::2]
            s0r, s0m, d0r, d0m = r[0] + r[2], m[0] + m[2], r[0] - r[2], m[0] - m[2]
            s1r, s1m, d1r, d1m = r[1] + r[3], m[1] + m[3], r[1] - r[3], m[1] - m[3]
            return (
                [s0r + s1r, d0r - d1m, s0r - s1r, d0r + d1m],
                [s0m + s1m, d0m + d1r, s0m - s1m, d0m - d1r],
            )

        er, em = four(0)
        ar, am = four(1)
        br = [ar[0], (ar[1] - am[1]) * c, -am[2], -(ar[3] + am[3]) * c]
        bm = [am[0], (ar[1] + am[1]) * c, ar[2], (ar[3] - am[3]) * c]
        for b in range(4):
            store(b * sub + row, (er[b] + br[b]) * scale, (em[b] + bm[b]) * scale)
        return carry

    lax.fori_loop(0, sub // ROWS, gather, 0)


def fused_kernel(
    g_ref, inj_ref, w_ref, mask_ref, fwd_hbm, inv_hbm, out_ref,
    g_buf, send, rx, lo, hi, y, fwd, inv, z, t, v,
    g_sem, tab_sem, own_sem, a_send, a_recv, up_send, up_recv, down_send, down_recv,
    ret_own, ret_send, ret_recv,
):
    chunks, devices, rows, count, lanes = rx.shape
    energies = devices * count
    pairs = rows // 2
    cols = rows * lanes // 2
    block = g_buf.shape[2]
    groups = a_send.shape[1]
    span = count // groups
    me = lax.axis_index("energy")
    slab = lax.axis_index("slab")
    slabs = lax.axis_size("slab")
    has_up = slab < slabs - 1
    has_down = slab > 0

    def g_copy(i):
        start = pl.multiple_of(i * block, block)
        return pltpu.make_async_copy(
            g_ref.at[:, pl.ds(start, block)], g_buf.at[i % 2], g_sem.at[i % 2]
        )

    g_copy(0).start()
    fwd_copy = pltpu.make_async_copy(fwd_hbm, fwd, tab_sem.at[0])
    inv_copy = pltpu.make_async_copy(inv_hbm, inv, tab_sem.at[1])

    barrier = pltpu.get_barrier_semaphore()

    def greet(k, carry):
        pl.semaphore_signal(
            barrier, inc=1, device_id=((me + k) % devices, slab), device_id_type=MESH
        )
        return carry

    lax.fori_loop(1, devices, greet, 0)

    @pl.when(has_up)
    def _():
        pl.semaphore_signal(barrier, inc=1, device_id=(me, slab + 1), device_id_type=MESH)

    @pl.when(has_down)
    def _():
        pl.semaphore_signal(barrier, inc=1, device_id=(me, slab - 1), device_id_type=MESH)

    peers = devices - 1 + jnp.where(has_up, 1, 0) + jnp.where(has_down, 1, 0)
    pl.semaphore_wait(barrier, peers)

    def when_range(g):
        return pl.ds(pl.multiple_of(g * span, ROWS), span)

    def tile_copy(c, g, source, target, peer):
        part = when_range(g)
        return pltpu.make_async_remote_copy(
            src_ref=send.at[target, pl.ds(c * rows, rows), part],
            dst_ref=rx.at[c, source, :, part],
            send_sem=a_send.at[c, g, target],
            recv_sem=a_recv.at[c, g, source],
            device_id=(peer, slab),
            device_id_type=MESH,
        )

    def own_copy(c, g):
        part = when_range(g)
        return pltpu.make_async_copy(
            send.at[me, pl.ds(c * rows, rows), part], rx.at[c, me, :, part], own_sem.at[c, g]
        )

    def send_group(c, g):
        def one(k, carry):
            to = (me + k) % devices
            tile_copy(c, g, me, to, to).start()
            return carry

        lax.fori_loop(1, devices, one, 0)
        own_copy(c, g).start()

    def halo_copy(c, g, up):
        part = when_range(g)
        return pltpu.make_async_remote_copy(
            src_ref=rx.at[c, :, :, part],
            dst_ref=(lo if up else hi).at[c, :, :, part],
            send_sem=(up_send if up else down_send).at[c, g],
            recv_sem=(up_recv if up else down_recv).at[c, g],
            device_id=(me, slab + 1 if up else slab - 1),
            device_id_type=MESH,
        )

    def forward_group(c, g):
        def one(k, carry):
            source = (me + devices - k) % devices
            tile_copy(c, g, source, source, source).wait_recv()
            return carry

        lax.fori_loop(1, devices, one, 0)
        own_copy(c, g).wait()

        @pl.when(has_up)
        def _():
            halo_copy(c, g, True).start()

        @pl.when(has_down)
        def _():
            halo_copy(c, g, False).start()

    def wait_halos(c):
        def one(g, carry):
            @pl.when(has_down)
            def _():
                halo_copy(c, g, True).wait_recv()

            @pl.when(has_up)
            def _():
                halo_copy(c, g, False).wait_recv()

            return carry

        lax.fori_loop(0, groups, one, 0)

    steps = span // block
    early = min(2, chunks)

    def lesser_group(g, carry):
        def step(b, inner):
            i = g * steps + b

            @pl.when(i + 1 < groups * steps)
            def _():
                g_copy(i + 1).start()

            g_copy(i).wait()
            result = lesser_block(g_buf[i % 2], inj_ref[...])
            start = pl.multiple_of(i * block, block)
            send[:, :, pl.ds(start, block), :] = result.reshape(
                devices, chunks * rows, block, lanes
            )
            return inner

        lax.fori_loop(0, steps, step, 0)
        for c in range(early):
            send_group(c, g)

        @pl.when(g > 0)
        def _():
            forward_group(0, g - 1)

        return carry

    @pl.when(slab == 0)
    def _():
        lo[...] = jnp.zeros_like(lo)

    @pl.when(slab == slabs - 1)
    def _():
        hi[...] = jnp.zeros_like(hi)

    fwd_copy.start()
    inv_copy.start()
    lax.fori_loop(0, groups, lesser_group, 0)
    for c in range(early, chunks):
        lax.fori_loop(0, groups, lambda g, carry: (send_group(c, g), carry)[1], 0)
    forward_group(0, groups - 1)
    fwd_copy.wait()
    inv_copy.wait()

    def both(ref, c, p):
        parts = [ref[c, :, 2 * p + a].reshape(energies, lanes) for a in range(2)]
        return jnp.concatenate(parts, axis=1)

    def return_copy(c, source, target, peer):
        at = pl.multiple_of(source * (chunks * cols) + c * cols, 128)
        return pltpu.make_async_remote_copy(
            src_ref=y.at[c, target],
            dst_ref=out_ref.at[:, :, pl.ds(at, cols)],
            send_sem=ret_send.at[c, target],
            recv_sem=ret_recv.at[c, source],
            device_id=(peer, slab),
            device_id_type=MESH,
        )

    def return_own(c):
        at = pl.multiple_of(me * (chunks * cols) + c * cols, 128)
        return pltpu.make_async_copy(
            y.at[c, me], out_ref.at[:, :, pl.ds(at, cols)], ret_own.at[c]
        )

    scale = energies**-0.5 / (2 * energies)
    def chunk(c, none):
        wait_halos(c)
        for p in range(pairs):
            mix(
                both(rx, c, p),
                both(lo, c, p),
                both(hi, c, p),
                mask_ref,
                lambda o, q: w_ref[c * pairs + p, pl.ds(o * 2 + q, 1), :],
                z,
            )
            split_pair(z, t, p, pairs)

        def store(row, real, imag):
            dest = row // count
            inside = pl.multiple_of(row % count, ROWS)
            y[c, dest, 0, pl.ds(inside, ROWS), :] = real.astype(BF16)
            y[c, dest, 1, pl.ds(inside, ROWS), :] = imag.astype(BF16)

        def ahead(g):
            @pl.when(c + 1 < chunks)
            def _():
                forward_group(c + 1, g)

        hooks = [functools.partial(ahead, g) for g in range(groups)]
        convolve(t, fwd, inv, v, store, scale, hooks)

        def give(k, carry):
            to = (me + k) % devices
            return_copy(c, me, to, to).start()
            return carry

        lax.fori_loop(1, devices, give, 0)
        return_own(c).start()
        return none

    lax.fori_loop(0, chunks, chunk, 0)

    def close(c, none):
        return_own(c).wait()

        def finish(k, carry):
            peer = (me + k) % devices
            return_copy(c, peer, peer, peer).wait()
            return carry

        lax.fori_loop(1, devices, finish, 0)

        def drain(g, carry):
            def one(k, inner):
                to = (me + k) % devices
                tile_copy(c, g, me, to, to).wait_send()
                return inner

            lax.fori_loop(1, devices, one, 0)

            @pl.when(has_up)
            def _():
                halo_copy(c, g, True).wait_send()

            @pl.when(has_down)
            def _():
                halo_copy(c, g, False).wait_send()

            return carry

        lax.fori_loop(0, groups, drain, 0)
        return none

    lax.fori_loop(0, chunks, close, 0)


def fused_call(green, inject, weights, masks, fwd, inv, devices):
    _, count, window, width = green.shape
    energies = devices * count
    local_rows = window // devices
    chunks = max(1, local_rows // 2)
    rows = local_rows // chunks
    lanes = 2 * window
    cols = rows * lanes // 2
    sub = 2 * energies // RADIX
    groups = max(1, count // 48)
    vmem = pl.BlockSpec(memory_space=pltpu.VMEM)
    hbm = pl.BlockSpec(memory_space=pl.ANY)
    dma = pltpu.SemaphoreType.DMA
    slots = pltpu.VMEM((chunks, devices, rows, count, lanes), BF16)
    return pl.pallas_call(
        fused_kernel,
        in_specs=[hbm, vmem, vmem, vmem, hbm, hbm],
        out_specs=hbm,
        out_shape=jax.ShapeDtypeStruct((2, count, window * window), BF16),
        scratch_shapes=[
            pltpu.VMEM((2, 2, ROWS, window, width), BF16),
            pltpu.VMEM((devices, local_rows, count, lanes), BF16),
            slots,
            slots,
            slots,
            pltpu.VMEM((chunks, devices, 2, count, cols), BF16),
            pltpu.VMEM(fwd.shape, BF16),
            pltpu.VMEM(inv.shape, BF16),
            pltpu.VMEM((2, energies, 2 * lanes), F32),
            pltpu.VMEM((RADIX, 2 * sub, 2 * cols), BF16),
            pltpu.VMEM((RADIX, 2 * sub, cols), F32),
            dma((2,)),
            dma((2,)),
            dma((chunks, groups)),
            dma((chunks, groups, devices)),
            dma((chunks, groups, devices)),
            dma((chunks, groups)),
            dma((chunks, groups)),
            dma((chunks, groups)),
            dma((chunks, groups)),
            dma((chunks,)),
            dma((chunks, devices)),
            dma((chunks, devices)),
        ],
        compiler_params=pltpu.CompilerParams(
            vmem_limit_bytes=63 * 2**20, collective_id=0, has_side_effects=True
        ),
        cost_estimate=pl.CostEstimate(
            flops=2 * count * window * width * (2 * width + 4 * window)
            + 2 * RADIX * 4 * sub * sub * 3 * cols * chunks,
            bytes_accessed=48 * 2**20,
            transcendentals=0,
        ),
        name="fused",
    )(green, inject, weights, masks, fwd, inv)


def pair_weights(neighbour_ids, coupling, window):
    tiles = neighbour_ids.shape[0]
    candidates = lax.iota(jnp.int32, 3 * GROUP)
    matches = (neighbour_ids[:, :, None] == candidates).astype(F32)
    weights = jnp.sum(matches * coupling[:, :, None], axis=1)
    per_pair = 2 * window // TILE_ENTRIES
    weights = weights.reshape(tiles // per_pair, per_pair, 3 * GROUP).transpose(0, 2, 1)
    lanes = jnp.repeat(weights, TILE_ENTRIES, axis=2)
    lanes = jnp.concatenate([lanes, lanes], axis=2)
    return jnp.pad(lanes, ((0, 0), (0, 2), (0, 0)))


def local(g_rows, injection, neighbour_ids, coupling):
    green = g_rows[:, :, 0]
    devices = lax.axis_size("energy")
    window = green.shape[2]
    count = green.shape[1]
    weights = pair_weights(neighbour_ids[0], coupling[0], window)
    masks = jnp.asarray(pair_masks(window))
    fwd, inv = (jnp.asarray(t) for t in dft_tables(devices * count))
    out = fused_call(green, injection[0], weights, masks, fwd, inv, devices)
    return out.reshape(2, count, 1, window * window)


def solution(mesh):
    in_specs = (
        P(None, "energy", "slab", None, None),
        P("slab", None, None),
        P("slab", "energy", None),
        P("slab", "energy", None),
    )
    out_specs = P(None, "energy", "slab", None)
    return jax.shard_map(local, mesh=mesh, in_specs=in_specs, out_specs=out_specs, check_vma=False)
```
